512 devices in a mesh: seq: 128 (over y, z, core), head: 4 (over x).
Axes of the slice: x: 4, y: 8, z: 8, core: 2. Of those that a mesh axis runs over, the one named last changes fastest.
Arguments:
- queries: bfloat16 [16384, 2048], P('seq', 'head'), may hold values from -18 to 18
- keys: bfloat16 [16384, 2048], P('seq', 'head'), may hold values from -12 to 12
- values: bfloat16 [16384, 2048], P('seq', 'head'), may hold values from -12 to 12
- norm_gain: float32 [2048], P('head'), may hold values from 0.1 to 1.9
- out_weight: bfloat16 [2048, 2048], P('head'), may hold values from -0.1875 to 0.1875
Outputs:
- mixed: bfloat16 [16384, 2048], P('seq', 'head')
The draws below stay inside these ranges and needn't reach their ends.
All inputs are finite; a program needn't handle non-finite values.
Results may differ from the reference program's by a relative error of at most 0.015.
Values may be sent and summed in bfloat16 or wider, within the bound.
No kernel may reach another device: no remote copies, remote signals or barrier semaphores. Data moves between devices by JAX's collectives and lax.ppermute only.
A program may use at most 64 MiB of HBM per device.

```python
import math
import jax
import jax.numpy as jnp
from jax import lax

D = 2048
HEADS = 16
HEAD_DIM = 128
BLOCK = 64
SEQ = 16384


def draw_queries(key, part):
    own_key = jax.random.fold_in(key, 11)
    result = jax.random.truncated_normal(own_key, -6.0, 6.0, (SEQ, HEADS * HEAD_DIM), jnp.float32)
    return result.astype(jnp.bfloat16)


def draw_keys(key, part):
    own_key = jax.random.fold_in(key, 17)
    result = jax.random.truncated_normal(own_key, -6.0, 6.0, (SEQ, HEADS * HEAD_DIM), jnp.float32)
    return result.astype(jnp.bfloat16)


def draw_values(key, part):
    own_key = jax.random.fold_in(key, 23)
    head_of = (jnp.arange(HEADS * HEAD_DIM) // HEAD_DIM).astype(jnp.float32)
    column_scale = 0.5 * 4.0 ** (head_of / (HEADS - 1))
    result = jax.random.truncated_normal(own_key, -6.0, 6.0, (SEQ, HEADS * HEAD_DIM), jnp.float32) * column_scale
    return result.astype(jnp.bfloat16)


def spiked(values, rng, source, target, parts, factor):
    def block_of(axis_at):
        return (jnp.arange(values.shape[axis_at]) // (values.shape[axis_at] // parts)).reshape((-1,) + (1,) * (values.ndim - 1 - axis_at))

    first = jax.random.permutation(rng, parts)[block_of(target)]
    far = (block_of(target) + parts // 2) % parts
    return jnp.where((block_of(source) == first) | (block_of(source) == far), factor * values, values)


def block_levels(stream_key, dims, shards, smallest, top_value):
    def one(dim, blocks):
        heights = jax.random.uniform(jax.random.fold_in(jax.random.fold_in(stream_key, 6), dim), (blocks,), jnp.float32, smallest / len(shards), top_value / len(shards))
        return jnp.repeat(jnp.exp(heights), dims[dim] // blocks).reshape((-1,) + (1,) * (len(dims) - dim - 1))

    gain = one(*shards[0])
    for cut in shards[1:]:
        gain = gain * one(*cut)
    return gain


def noise_with(key, dims, deviation, bound, cuts, heavy, held_as=jnp.bfloat16):
    values = deviation * jax.random.normal(key, dims, jnp.float32)
    if cuts:
        values = values * block_levels(key, dims, cuts, -0.22, 0.18)
    return jnp.clip(spiked(values, jax.random.fold_in(key, 3), *heavy), -bound, bound).astype(held_as)


def setup_inputs(seed: int = 0) -> dict:
    key_list = jax.random.split(jax.random.key(seed), 6)
    return {
        "queries": draw_queries(jax.random.fold_in(key_list[5], 71), 0),
        "keys": draw_keys(jax.random.fold_in(key_list[5], 71), 0),
        "values": draw_values(jax.random.fold_in(key_list[5], 71), 0),
        "norm_gain": jnp.clip(1.0 + 0.18 * jax.random.normal(key_list[3], (HEADS * HEAD_DIM,), jnp.float32), 0.1, 1.9),
        "out_weight": noise_with(key_list[4], (HEADS * HEAD_DIM, D), (HEADS * HEAD_DIM) ** -0.5, 0.1875, ((0, 4),), (0, 1, 4, 2.0)),
    }


inv_root = 1.0 / math.sqrt(2.0)
eps_value = 1e-06

def restrict(blocked):
    pairs = blocked.reshape(blocked.shape[:-2] + (blocked.shape[-2] // 2, 2, blocked.shape[-1]))
    summed = pairs[..., 0, :].astype(jnp.float32) + pairs[..., 1, :].astype(jnp.float32)
    return lax.optimization_barrier((summed * inv_root).astype(jnp.bfloat16))

def partial_softmax(query_rows, key_rows, value_rows, allowed, head_count):
    query_heads = query_rows.reshape(query_rows.shape[:-1] + (head_count, -1)).astype(jnp.float32)
    key_heads = key_rows.reshape(key_rows.shape[:-1] + (head_count, -1)).astype(jnp.float32)
    value_heads = value_rows.reshape(value_rows.shape[:-1] + (head_count, -1)).astype(jnp.float32)
    scaling = 1.0 / math.sqrt(query_heads.shape[-1])
    scores = jnp.einsum('...rhd,...whd->...hrw', query_heads, key_heads) * scaling
    masked = jnp.where(allowed[..., None, :, :], scores, -jnp.inf)
    highest = lax.optimization_barrier(jnp.max(masked, axis=-1))
    weights = jnp.exp(masked - highest[..., None])
    totals = lax.optimization_barrier(jnp.sum(weights, axis=-1))
    rounded = lax.optimization_barrier(weights.astype(jnp.bfloat16)).astype(jnp.float32)
    summed = jnp.einsum('...hrw,...whd->...rhd', rounded, value_heads)
    return (jnp.swapaxes(highest, -1, -2), jnp.swapaxes(totals, -1, -2), summed)

def merge_pieces(current, incoming):
    largest = jnp.maximum(current[0], incoming[0])
    older = jnp.exp(current[0] - largest)
    newer = jnp.exp(incoming[0] - largest)
    return (largest, current[1] * older + incoming[1] * newer, current[2] * older[..., None] + incoming[2] * newer[..., None])

def reference(queries, keys, values, norm_gain, out_weight):
    seq_length, features = queries.shape
    head_count = features // HEAD_DIM
    level_count = (seq_length // (4 * BLOCK)).bit_length() - 1

    def split_heads(array):
        return array.reshape(seq_length, head_count, HEAD_DIM).transpose(1, 0, 2)

    def one_head(operands):
        query_rows, key_rows, value_rows = operands
        leaf_blocks = seq_length // BLOCK
        stacked = jnp.stack([key_rows, value_rows])
        padded = jnp.pad(stacked, ((0, 0), (BLOCK, BLOCK), (0, 0)))
        windows = jnp.concatenate([padded[:, slot_index * BLOCK:slot_index * BLOCK + seq_length].reshape(2, leaf_blocks, BLOCK, HEAD_DIM) for slot_index in range(3)], axis=2)
        global_block = jnp.arange(leaf_blocks, dtype=jnp.int32)[:, None] + jnp.arange(3 * BLOCK, dtype=jnp.int32)[None, :] // BLOCK - 1
        leaf_valid = (global_block >= 0) & (global_block < leaf_blocks)
        near = partial_softmax(query_rows.reshape(leaf_blocks, BLOCK, HEAD_DIM), windows[0], windows[1], leaf_valid[:, None, :], 1)
        state = (near[0].reshape(seq_length, 1), near[1].reshape(seq_length, 1), near[2].reshape(seq_length, 1, HEAD_DIM))
        coarse_queries = query_rows
        coarse_pairs = stacked
        for level_id in range(1, level_count + 1):
            coarse_queries = restrict(coarse_queries)
            coarse_pairs = restrict(coarse_pairs)
            level_rows = seq_length >> level_id
            block_count = level_rows // BLOCK
            level_padded = jnp.pad(coarse_pairs, ((0, 0), (3 * BLOCK, 3 * BLOCK), (0, 0)))

            def blocks_at(offset):
                begin = (offset + 3) * BLOCK
                return level_padded[:, begin:begin + level_rows].reshape(2, block_count, BLOCK, HEAD_DIM)
            block_index = jnp.arange(block_count, dtype=jnp.int32)
            is_even = block_index % 2 == 0
            even_offsets = (-2, 2, 3)
            odd_offsets = (-3, -2, 2)
            even_window = jnp.concatenate([blocks_at(offset) for offset in even_offsets], axis=2)
            odd_window = jnp.concatenate([blocks_at(offset) for offset in odd_offsets], axis=2)
            window = jnp.where(is_even[None, :, None, None], even_window, odd_window)
            chosen_offsets = jnp.where(is_even[:, None], jnp.array(even_offsets, dtype=jnp.int32)[None, :], jnp.array(odd_offsets, dtype=jnp.int32)[None, :])
            target = block_index[:, None] + chosen_offsets
            inside = (target >= 0) & (target < block_count)
            level_valid = jnp.repeat(inside, BLOCK, axis=1)
            level_piece = partial_softmax(coarse_queries.reshape(block_count, BLOCK, HEAD_DIM), window[0], window[1], level_valid[:, None, :], 1)
            factor = 2 ** level_id
            level_piece = (jnp.repeat(level_piece[0].reshape(level_rows, 1), factor, axis=0), jnp.repeat(level_piece[1].reshape(level_rows, 1), factor, axis=0), jnp.repeat(level_piece[2].reshape(level_rows, 1, HEAD_DIM), factor, axis=0))
            state = merge_pieces(state, level_piece)
        return state[2][:, 0, :] / state[1][:, 0, None]
    attended = lax.map(one_head, (split_heads(queries), split_heads(keys), split_heads(values)))
    attended = attended.transpose(1, 0, 2).reshape(seq_length, features).astype(jnp.bfloat16)
    widened = lax.optimization_barrier(attended).astype(jnp.float32)
    mean_square = lax.optimization_barrier(jnp.sum(widened * widened, axis=1)) / features
    normed = (widened * lax.rsqrt(mean_square + eps_value)[:, None] * norm_gain).astype(jnp.bfloat16)
    return jnp.dot(normed, out_weight, preferred_element_type=jnp.float32).astype(jnp.bfloat16)
```

```python
import math

import jax
import jax.numpy as jnp
from jax import lax
from jax.experimental import pallas as pl
from jax.experimental.pallas import tpu as pltpu
from jax.sharding import Mesh
from jax.sharding import PartitionSpec as P

HEAD_DIM = 128
BLOCK = 64
QUADS = 32
TOKENS = 512
PAIR = 2 * HEAD_DIM
eps_value = 1e-06
inv_root = 1.0 / math.sqrt(2.0)
scaling = 1.0 / math.sqrt(HEAD_DIM)
NEG = -1e30
PARAMS = pltpu.CompilerParams(vmem_limit_bytes=48 * 1024 * 1024)
FULL = pltpu.CompilerParams(vmem_limit_bytes=60 * 1024 * 1024)
NEEDED = (
    (2, 3, 6, 4),
    (3, 6, 7, 4),
    (0, 4, 5, 6),
    (0, 1, 5, 6),
    (2, 6, 7, 0),
    (2, 3, 7, 0),
    (4, 0, 1, 2),
    (4, 5, 1, 2),
)


def pair_sums(rows, columns):
    out_row = lax.broadcasted_iota(jnp.int32, (rows, columns), 0)
    in_row = lax.broadcasted_iota(jnp.int32, (rows, columns), 1)
    return ((in_row >> 1) == out_row).astype(jnp.float32).astype(jnp.bfloat16)


def restrict(fine, matrix):
    summed = jnp.dot(matrix, fine, preferred_element_type=jnp.float32)
    return (summed * inv_root).astype(jnp.bfloat16)


def piece(query, key, value, allowed):
    scores = lax.dot_general(
        query, key, (((1,), (1,)), ((), ())), preferred_element_type=jnp.float32
    )
    scores = scores * scaling
    if allowed is not None:
        scores = jnp.where(allowed, scores, NEG)
    highest = jnp.max(scores, axis=1, keepdims=True)
    weights = jnp.exp(scores - highest)
    total = jnp.sum(weights, axis=1, keepdims=True)
    summed = jnp.dot(weights.astype(jnp.bfloat16), value, preferred_element_type=jnp.float32)
    shape = summed.shape
    return jnp.broadcast_to(highest, shape), jnp.broadcast_to(total, shape), summed


def attend(query, pairs, allowed):
    return piece(query, pairs[:, :HEAD_DIM], pairs[:, HEAD_DIM:], allowed)


def merge_pieces(current, incoming):
    largest = jnp.maximum(current[0], incoming[0])
    older = jnp.exp(current[0] - largest)
    newer = jnp.exp(incoming[0] - largest)
    return (
        largest,
        current[1] * older + incoming[1] * newer,
        current[2] * older + incoming[2] * newer,
    )


def spread(state, scratch, rows, factor):
    result = []
    for index, member in enumerate(state):
        for step in range(factor):
            scratch[index, pl.ds(step, rows, stride=factor), :] = member[:rows]
        result.append(scratch[index, : rows * factor, :])
    return tuple(result)


def third_mask(rows, valid):
    block = lax.broadcasted_iota(jnp.int32, (rows, 3 * BLOCK), 1) // BLOCK
    flags = [jnp.where(flag, 1, 0) for flag in valid]
    chosen = jnp.where(block == 0, flags[0], jnp.where(block == 1, flags[1], flags[2]))
    return chosen == 1


def begin_copies(copies, sems):
    started = [
        pltpu.make_async_copy(source, target, sems.at[index])
        for index, (source, target) in enumerate(copies)
    ]
    for copy in started:
        copy.start()
    return started


def wait_copies(started):
    for copy in started:
        copy.wait()


def my_place():
    return lax.axis_index("zl") * 2 + lax.axis_index("c")


def other_place(step):
    high, low = lax.axis_index("zl"), lax.axis_index("c")
    if step & 2:
        high = 1 - high
    if step & 1:
        low = 1 - low
    return high * 2 + low


def open_kernel(queries_ref, keys_ref, values_ref, column_ref, *refs):
    head_refs, pairs_ref, sems = refs[:4], refs[4], refs[5]
    copies = [(keys_ref, pairs_ref.at[:, :512]), (values_ref, pairs_ref.at[:, 512:])]
    for step, head_ref in enumerate(head_refs):
        begin = pl.multiple_of(other_place(step) * HEAD_DIM, HEAD_DIM)
        for index, ref in enumerate((queries_ref, keys_ref, values_ref)):
            columns = slice(index * HEAD_DIM, (index + 1) * HEAD_DIM)
            copies.append((ref.at[:, pl.ds(begin, HEAD_DIM)], head_ref.at[:, columns]))
    started = begin_copies(copies, sems)
    wait_copies(started[:2])
    first = restrict(pairs_ref[...], pair_sums(64, 128))
    third = restrict(restrict(first, pair_sums(32, 64)), pair_sums(16, 32))
    for row in range(8):
        column_ref[row] = third
    wait_copies(started[2:])


def column_kernel(row_ref, needed_ref, column_ref, *refs):
    out_ref = refs[-1]
    row = row_ref[0]
    chosen = [needed_ref[row * 4 + slot] for slot in range(4)]
    chosen.append(chosen[3] + 1)
    rest = jnp.concatenate([column_ref[source] for source in chosen], axis=0)
    fourth = restrict(rest, pair_sums(48, 80))
    fifth = restrict(fourth, pair_sums(32, 48))
    out_row = lax.broadcasted_iota(jnp.int32, (16, 32), 0)
    in_row = lax.broadcasted_iota(jnp.int32, (16, 32), 1)
    kept = (out_row < 12) & (in_row == out_row)
    halved = (out_row >= 12) & (((in_row - 12) >> 1) == out_row - 12)
    matrix = jnp.where(kept | halved, 1.0, 0.0).astype(jnp.bfloat16)
    tail = jnp.dot(matrix, fifth, preferred_element_type=jnp.float32)
    place = lax.broadcasted_iota(jnp.int32, tail.shape, 0)
    tail = jnp.where(place < 12, tail, tail * inv_root).astype(jnp.bfloat16)
    members = [column_ref[lax.rem(row + step + 7, 8)] for step in range(3)] + [tail]
    whole = jnp.concatenate(members, axis=0)
    for head in range(4):
        low = head * HEAD_DIM
        for group in range(4):
            out_ref[group * 4 + head, :, :HEAD_DIM] = whole[:, low : low + HEAD_DIM]
            out_ref[group * 4 + head, :, HEAD_DIM:] = whole[:, 512 + low : 512 + low + HEAD_DIM]


def prepare_kernel(own_ref, one_ref, two_ref, three_ref, *refs):
    x_ref, next_ref, prev_ref, query_ref, sems = refs
    copies = []
    for step, ref in enumerate((own_ref, one_ref, two_ref, three_ref)):
        begin = pl.multiple_of(other_place(step) * 128, 128)
        copies.append((ref, x_ref.at[pl.ds(begin, 128), :]))
    wait_copies(begin_copies(copies, sems))
    x = x_ref[...]
    next_ref[:64] = x[TOKENS - 64 :, HEAD_DIM:]
    prev_ref[:64] = x[:64, HEAD_DIM:]
    first = restrict(x, pair_sums(256, 512))
    next_ref[64:192] = first[128:, HEAD_DIM:]
    prev_ref[64:192] = first[:128, HEAD_DIM:]
    query_ref[:256] = first[:, :HEAD_DIM]
    second = restrict(first, pair_sums(128, 256))
    next_ref[192:] = second[:, HEAD_DIM:]
    prev_ref[192:] = second[:, HEAD_DIM:]
    query_ref[256:384] = second[:, :HEAD_DIM]
    third = restrict(second[:, :HEAD_DIM], pair_sums(64, 128))
    query_ref[384:448] = third
    fourth = restrict(third, pair_sums(32, 64))
    query_ref[448:480] = fourth
    fifth = restrict(fourth, pair_sums(16, 32))
    query_ref[480:496] = fifth
    query_ref[496:512] = restrict(fifth, pair_sums(16, 16))


def block_rows(array, blocks):
    return jnp.concatenate([array[block * BLOCK : (block + 1) * BLOCK] for block in blocks], axis=0)


def far_piece(query, pairs_ref, block, block_count, first=0):
    even = block % 2 == 0
    chosen = (
        jnp.where(even, block - 2, block - 3),
        jnp.where(even, block + 2, block - 2),
        jnp.where(even, block + 3, block + 2),
    )
    valid = [(target >= 0) & (target < block_count) for target in chosen]
    last = pairs_ref.shape[0] // BLOCK - 1
    parts = []
    for target in chosen:
        begin = pl.multiple_of(jnp.clip(target - first, 0, last) * BLOCK, BLOCK)
        parts.append(pairs_ref[pl.ds(begin, BLOCK), :])
    return attend(query, jnp.concatenate(parts, axis=0), third_mask(query.shape[0], valid))


def gather_levels(row, needed_ref, row_ref, third_ref, fourth_ref, fifth_ref, sixth_ref):
    wide, narrow = pair_sums(128, 256), pair_sums(64, 128)
    fifth_ref[...] = jnp.zeros_like(fifth_ref)
    for step in range(3):
        low, high = step * 256, step * 128
        rows = [row_ref[source, step * 16 : (step + 1) * 16] for source in range(16)]
        third = jnp.concatenate(rows, axis=0)
        third_ref[low : low + 256] = third
        fourth = restrict(third, wide)
        fourth_ref[high : high + 128] = fourth
        begin = pl.multiple_of(lax.rem(row + step + 7, 8) * 64, 64)
        fifth_ref[pl.ds(begin, 64), :] = restrict(fourth, narrow)
    tail = jnp.concatenate([row_ref[source, 48:64] for source in range(16)], axis=0)
    out_row = lax.broadcasted_iota(jnp.int32, (256, 256), 0)
    in_row = lax.broadcasted_iota(jnp.int32, (256, 256), 1)
    of_fifth = ((out_row & 63) >> 2) * 16 + (out_row >> 6) * 4 + (out_row & 3)
    of_sixth = ((out_row & 31) >> 1) * 16 + 12 + ((out_row >> 5) & 1) * 2 + (out_row & 1)
    source = jnp.where(out_row < 192, of_fifth, of_sixth)
    matrix = jnp.where(in_row == source, 1.0, 0.0).astype(jnp.bfloat16)
    ordered = jnp.dot(matrix, tail, preferred_element_type=jnp.float32).astype(jnp.bfloat16)
    for slot in range(3):
        begin = pl.multiple_of(needed_ref[row * 4 + slot] * 64, 64)
        fifth_ref[pl.ds(begin, 64), :] = ordered[slot * 64 : (slot + 1) * 64]
    for begin in range(0, 256, 128):
        sixth_ref[begin : begin + 128] = restrict(fifth_ref[2 * begin : 2 * begin + 256], wide)
    begin = pl.multiple_of(needed_ref[row * 4 + 3] * 32, 64)
    sixth_ref[pl.ds(begin, 64), :] = ordered[192:]


def inner_kernel(x_ref, inner_ref):
    x = x_ref[...]
    for block in range(1, 7):
        rows = slice(block * BLOCK, (block + 1) * BLOCK)
        keys = slice((block - 1) * BLOCK, (block + 2) * BLOCK)
        near = attend(x[rows, :HEAD_DIM], x[keys, HEAD_DIM:], None)
        for index, member in enumerate(near):
            inner_ref[index, rows] = member


def far_kernel(quad_ref, needed_ref, query_ref, row_hbm, far_ref, row_ref, *refs):
    *levels, scratch, sems = refs
    started = begin_copies(((row_hbm, row_ref),), sems)
    wait_copies(started)
    quad = quad_ref[0]
    row = quad // 4
    third_ref, fourth_ref, fifth_ref, sixth_ref = levels
    gather_levels(row, needed_ref, row_ref, third_ref, fourth_ref, fifth_ref, sixth_ref)
    state = far_piece(query_ref[496:512], sixth_ref, row // 2, 4)
    state = spread(state, scratch, 8, 2)
    state = merge_pieces(far_piece(query_ref[480:496], fifth_ref, row, 8), state)
    state = spread(state, scratch, 16, 2)
    fourth = far_piece(query_ref[448:480], fourth_ref, quad // 2, 16, 2 * row - 2)
    state = spread(merge_pieces(fourth, state), scratch, 32, 2)
    third = far_piece(query_ref[384:448], third_ref, quad, 32, 4 * row - 4)
    for index, member in enumerate(merge_pieces(third, state)):
        for step in range(2):
            far_ref[index, pl.ds(step, 64, stride=2), :] = member


def attend_kernel(
    quad_ref, x_ref, query_ref, far_ref, inner_ref, prev_hbm, next_hbm, out_ref, *refs
):
    prev_ref, next_ref, scratch, sems = refs
    started = begin_copies(((prev_hbm, prev_ref), (next_hbm, next_ref)), sems)
    wait_copies(started)
    quad = quad_ref[0]
    has_prev = quad > 0
    has_next = quad < QUADS - 1
    x = x_ref[...]
    state = tuple(far_ref[index] for index in range(3))
    prev, later = prev_ref[...], next_ref[...]
    rim = jnp.concatenate([prev[192:], later[192:]], axis=0)
    pieces = []
    for block, chosen, valid in (
        (0, (0, 2, 3), (has_prev, has_next, has_next)),
        (1, (0, 1, 3), (has_prev, has_prev, has_next)),
    ):
        rows = slice(256 + block * BLOCK, 256 + (block + 1) * BLOCK)
        pieces.append(attend(query_ref[rows], block_rows(rim, chosen), third_mask(BLOCK, valid)))
    second = tuple(jnp.concatenate(members, axis=0) for members in zip(*pieces))
    state = spread(merge_pieces(second, state), scratch, 128, 2)
    own = restrict(x[:, HEAD_DIM:], pair_sums(256, 512))
    rim = jnp.concatenate([prev[64:192], own, later[64:192]], axis=0)
    pieces = []
    for block, chosen, valid in (
        (0, (0, 4, 5), (has_prev, True, True)),
        (1, (0, 1, 5), (has_prev, has_prev, True)),
        (2, (2, 6, 7), (True, has_next, has_next)),
        (3, (2, 3, 7), (True, True, has_next)),
    ):
        rows = slice(block * BLOCK, (block + 1) * BLOCK)
        pieces.append(attend(query_ref[rows], block_rows(rim, chosen), third_mask(BLOCK, valid)))
    first = tuple(jnp.concatenate(members, axis=0) for members in zip(*pieces))
    state = spread(merge_pieces(first, state), scratch, 256, 2)
    rim = jnp.concatenate([prev[:64], x[:, HEAD_DIM:], later[:64]], axis=0)
    for block in range(8):
        rows = slice(block * BLOCK, (block + 1) * BLOCK)
        if block in (0, 7):
            valid = (has_prev, True, True) if block == 0 else (True, True, has_next)
            keys = rim[block * BLOCK : (block + 3) * BLOCK]
            near = attend(x[rows, :HEAD_DIM], keys, third_mask(BLOCK, valid))
        else:
            near = tuple(inner_ref[index, rows] for index in range(3))
        _, total, summed = merge_pieces(near, tuple(member[rows] for member in state))
        out_ref[rows] = (summed / total).astype(jnp.bfloat16)


def project_kernel(attended_ref, weight_ref, gain_ref, out_ref):
    rows = jnp.concatenate([attended_ref[head] for head in range(4)], axis=1)
    widened = rows.astype(jnp.float32)
    squares = jnp.sum(widened * widened, axis=1, keepdims=True)
    squares = jnp.transpose(jnp.broadcast_to(squares, (128, 128)))[:16]
    coarse = squares.astype(jnp.bfloat16)
    rest = (squares - coarse.astype(jnp.float32)).astype(jnp.bfloat16)
    gained = (widened * gain_ref[...]).astype(jnp.bfloat16)
    for target in range(4):
        columns = slice(target * 512, (target + 1) * 512)
        product = jnp.dot(gained, weight_ref[:, columns], preferred_element_type=jnp.float32)
        out_ref[target, :128] = product.astype(jnp.bfloat16)
        out_ref[target, 128:, :128] = coarse
        out_ref[target, 128:, 128:256] = rest
        out_ref[target, 128:, 256:] = jnp.zeros((16, 256), jnp.bfloat16)


def sum_kernel(parts_ref, out_ref):
    summed = jnp.zeros((128, 512), jnp.float32)
    squares = jnp.zeros((16, 128), jnp.float32)
    for source in range(4):
        summed = summed + parts_ref[source, :128].astype(jnp.float32)
        squares = squares + parts_ref[source, 128:, :128].astype(jnp.float32)
        squares = squares + parts_ref[source, 128:, 128:256].astype(jnp.float32)
    mean_square = jnp.transpose(jnp.broadcast_to(squares[:1], (128, 128)))[:, :1] * (1.0 / 2048)
    out_ref[...] = (summed * lax.rsqrt(mean_square + eps_value)).astype(jnp.bfloat16)


def shift_pairs(by):
    return [
        (quad * 4 + place, (quad + by) * 4 + place)
        for quad in range(QUADS)
        if 0 <= quad + by < QUADS
        for place in range(4)
    ]


def exchange_pairs(step):
    return [(device, device ^ step) for device in range(4 * QUADS)]


ANYWHERE = pl.BlockSpec(memory_space=pl.ANY)
SCALARS = pl.BlockSpec(memory_space=pltpu.SMEM)


def vmem(count):
    return [pl.BlockSpec(memory_space=pltpu.VMEM)] * count


def bf16(*shape):
    return jax.ShapeDtypeStruct(shape, jnp.bfloat16)


def shards(queries, keys, values, norm_gain, out_weight):
    line = ("y", "zh", "zl", "c")
    row = lax.axis_index("y").astype(jnp.int32)
    quad = row * 4 + lax.axis_index("zh").astype(jnp.int32)
    row, quad = row.reshape(1), quad.reshape(1)
    needed = jnp.array([slot for slots in NEEDED for slot in slots], jnp.int32)
    column, *heads = pl.pallas_call(
        open_kernel,
        out_shape=[bf16(8, 16, 1024)] + [bf16(128, 3 * HEAD_DIM)] * 4,
        in_specs=[ANYWHERE] * 3,
        out_specs=vmem(5),
        scratch_shapes=[
            pltpu.VMEM((128, 1024), jnp.bfloat16),
            pltpu.SemaphoreType.DMA((14,)),
        ],
        compiler_params=FULL,
    )(queries, keys, values)
    column = lax.all_to_all(column, "y", 0, 0, tiled=True)
    for step in range(1, 4):
        heads[step] = lax.ppermute(heads[step], line, exchange_pairs(step))
    row_parts = pl.pallas_call(
        column_kernel,
        out_shape=bf16(16, 64, PAIR),
        in_specs=[SCALARS] * 2 + vmem(1) + [ANYWHERE] * 3,
        out_specs=vmem(1)[0],
        compiler_params=PARAMS,
    )(row, needed, column, *heads[1:])
    row_all = lax.all_to_all(row_parts, ("zh", "zl", "c"), 0, 0, tiled=True)
    x, to_next, to_prev, coarse_queries = pl.pallas_call(
        prepare_kernel,
        out_shape=[
            bf16(TOKENS, 3 * HEAD_DIM),
            bf16(320, PAIR),
            bf16(320, PAIR),
            bf16(512, HEAD_DIM),
        ],
        in_specs=[ANYWHERE] * 4,
        out_specs=vmem(4),
        scratch_shapes=[pltpu.SemaphoreType.DMA((4,))],
        compiler_params=PARAMS,
    )(*heads)
    from_prev = lax.ppermute(to_next, line, shift_pairs(1))
    from_next = lax.ppermute(to_prev, line, shift_pairs(-1))
    inner = pl.pallas_call(
        inner_kernel,
        out_shape=jax.ShapeDtypeStruct((3, TOKENS, HEAD_DIM), jnp.float32),
        in_specs=vmem(1),
        out_specs=vmem(1)[0],
        compiler_params=PARAMS,
    )(x)
    far = pl.pallas_call(
        far_kernel,
        out_shape=jax.ShapeDtypeStruct((3, 128, HEAD_DIM), jnp.float32),
        in_specs=[SCALARS] * 2 + vmem(1) + [ANYWHERE],
        out_specs=vmem(1)[0],
        scratch_shapes=[
            pltpu.VMEM((16, 64, PAIR), jnp.bfloat16),
            pltpu.VMEM((768, PAIR), jnp.bfloat16),
            pltpu.VMEM((384, PAIR), jnp.bfloat16),
            pltpu.VMEM((512, PAIR), jnp.bfloat16),
            pltpu.VMEM((256, PAIR), jnp.bfloat16),
            pltpu.VMEM((3, 128, HEAD_DIM), jnp.float32),
            pltpu.SemaphoreType.DMA((1,)),
        ],
        compiler_params=PARAMS,
    )(quad, needed, coarse_queries, row_all)
    attended = pl.pallas_call(
        attend_kernel,
        out_shape=bf16(TOKENS, HEAD_DIM),
        in_specs=[SCALARS] + vmem(4) + [ANYWHERE] * 2,
        out_specs=vmem(1)[0],
        scratch_shapes=[
            pltpu.VMEM((320, PAIR), jnp.bfloat16),
            pltpu.VMEM((320, PAIR), jnp.bfloat16),
            pltpu.VMEM((3, TOKENS, HEAD_DIM), jnp.float32),
            pltpu.SemaphoreType.DMA((2,)),
        ],
        compiler_params=PARAMS,
    )(quad, x, coarse_queries, far, inner, from_prev, from_next)
    own = lax.all_to_all(attended.reshape(4, 128, HEAD_DIM), ("zl", "c"), 0, 0, tiled=True)
    products = pl.pallas_call(
        project_kernel,
        out_shape=bf16(4, 144, 512),
        in_specs=vmem(3),
        out_specs=vmem(1)[0],
        compiler_params=PARAMS,
    )(own, out_weight, norm_gain.reshape(1, 512))
    parts = lax.all_to_all(products, "x", 0, 0, tiled=True)
    return pl.pallas_call(
        sum_kernel,
        out_shape=bf16(128, 512),
        in_specs=vmem(1),
        out_specs=vmem(1)[0],
        compiler_params=PARAMS,
    )(parts)


def solution(mesh):
    grid = Mesh(mesh.devices.reshape(8, 4, 2, 2, 4), ("y", "zh", "zl", "c", "x"))
    split = P(("y", "zh", "zl", "c"), "x")
    return jax.shard_map(
        shards,
        mesh=grid,
        in_specs=(split, split, split, P("x"), P("x", None)),
        out_specs=split,
        check_vma=False,
    )
```

```python
import math

import jax
import jax.numpy as jnp
from jax import lax
from jax.experimental import pallas as pl
from jax.experimental.pallas import tpu as pltpu
from jax.sharding import Mesh
from jax.sharding import PartitionSpec as P

HEAD_DIM = 128
BLOCK = 64
QUADS = 32
TOKENS = 512
PAIR = 2 * HEAD_DIM
eps_value = 1e-06
inv_root = 1.0 / math.sqrt(2.0)
scaling = 1.0 / math.sqrt(HEAD_DIM)
NEG = -1e30
PARAMS = pltpu.CompilerParams(vmem_limit_bytes=48 * 1024 * 1024)
FULL = pltpu.CompilerParams(vmem_limit_bytes=60 * 1024 * 1024)
NEEDED = (
    (2, 3, 6, 4),
    (3, 6, 7, 4),
    (0, 4, 5, 6),
    (0, 1, 5, 6),
    (2, 6, 7, 0),
    (2, 3, 7, 0),
    (4, 0, 1, 2),
    (4, 5, 1, 2),
)


def pair_sums(rows, columns):
    out_row = lax.broadcasted_iota(jnp.int32, (rows, columns), 0)
    in_row = lax.broadcasted_iota(jnp.int32, (rows, columns), 1)
    return ((in_row >> 1) == out_row).astype(jnp.float32).astype(jnp.bfloat16)


def restrict(fine, matrix):
    summed = jnp.dot(matrix, fine, preferred_element_type=jnp.float32)
    return (summed * inv_root).astype(jnp.bfloat16)


def piece(query, key, value, allowed):
    scores = lax.dot_general(
        query, key, (((1,), (1,)), ((), ())), preferred_element_type=jnp.float32
    )
    scores = scores * scaling
    if allowed is not None:
        scores = jnp.where(allowed, scores, NEG)
    highest = jnp.max(scores, axis=1, keepdims=True)
    weights = jnp.exp(scores - highest)
    total = jnp.sum(weights, axis=1, keepdims=True)
    summed = jnp.dot(weights.astype(jnp.bfloat16), value, preferred_element_type=jnp.float32)
    shape = summed.shape
    return jnp.broadcast_to(highest, shape), jnp.broadcast_to(total, shape), summed


def attend(query, pairs, allowed):
    return piece(query, pairs[:, :HEAD_DIM], pairs[:, HEAD_DIM:], allowed)


def merge_pieces(current, incoming):
    largest = jnp.maximum(current[0], incoming[0])
    older = jnp.exp(current[0] - largest)
    newer = jnp.exp(incoming[0] - largest)
    return (
        largest,
        current[1] * older + incoming[1] * newer,
        current[2] * older + incoming[2] * newer,
    )


def spread(state, scratch, rows, factor):
    result = []
    for index, member in enumerate(state):
        for step in range(factor):
            scratch[index, pl.ds(step, rows, stride=factor), :] = member[:rows]
        result.append(scratch[index, : rows * factor, :])
    return tuple(result)


def third_mask(rows, valid):
    block = lax.broadcasted_iota(jnp.int32, (rows, 3 * BLOCK), 1) // BLOCK
    flags = [jnp.where(flag, 1, 0) for flag in valid]
    chosen = jnp.where(block == 0, flags[0], jnp.where(block == 1, flags[1], flags[2]))
    return chosen == 1


def needed_row(row, slot):
    chosen = NEEDED[0][slot]
    for index in range(1, 8):
        chosen = jnp.where(row == index, NEEDED[index][slot], chosen)
    return chosen


def my_quad():
    return lax.axis_index("y") * 4 + lax.axis_index("zh")


def begin_copies(copies, sems):
    started = [
        pltpu.make_async_copy(source, target, sems.at[index])
        for index, (source, target) in enumerate(copies)
    ]
    for copy in started:
        copy.start()
    return started


def wait_copies(started):
    for copy in started:
        copy.wait()


def other_place(step):
    high, low = lax.axis_index("zl"), lax.axis_index("c")
    if step & 2:
        high = 1 - high
    if step & 1:
        low = 1 - low
    return high * 2 + low


def open_kernel(queries_ref, keys_ref, values_ref, column_ref, *refs):
    head_refs, pairs_ref, sems = refs[:4], refs[4], refs[5]
    copies = [(keys_ref, pairs_ref.at[:, :512]), (values_ref, pairs_ref.at[:, 512:])]
    for step, head_ref in enumerate(head_refs):
        begin = pl.multiple_of(other_place(step) * HEAD_DIM, HEAD_DIM)
        for index, ref in enumerate((queries_ref, keys_ref, values_ref)):
            columns = slice(index * HEAD_DIM, (index + 1) * HEAD_DIM)
            copies.append((ref.at[:, pl.ds(begin, HEAD_DIM)], head_ref.at[:, columns]))
    started = begin_copies(copies, sems)
    wait_copies(started[:2])
    first = restrict(pairs_ref[...], pair_sums(64, 128))
    third = restrict(restrict(first, pair_sums(32, 64)), pair_sums(16, 32))
    for row in range(8):
        column_ref[row] = third
    wait_copies(started[2:])


def column_kernel(column_ref, *refs):
    out_ref = refs[-1]
    row = lax.axis_index("y")
    chosen = [needed_row(row, slot) for slot in range(4)]
    chosen.append(chosen[3] + 1)
    rest = jnp.concatenate([column_ref[source] for source in chosen], axis=0)
    fourth = restrict(rest, pair_sums(48, 80))
    fifth = restrict(fourth, pair_sums(32, 48))
    out_row = lax.broadcasted_iota(jnp.int32, (16, 32), 0)
    in_row = lax.broadcasted_iota(jnp.int32, (16, 32), 1)
    kept = (out_row < 12) & (in_row == out_row)
    halved = (out_row >= 12) & (((in_row - 12) >> 1) == out_row - 12)
    matrix = jnp.where(kept | halved, 1.0, 0.0).astype(jnp.bfloat16)
    tail = jnp.dot(matrix, fifth, preferred_element_type=jnp.float32)
    place = lax.broadcasted_iota(jnp.int32, tail.shape, 0)
    tail = jnp.where(place < 12, tail, tail * inv_root).astype(jnp.bfloat16)
    members = [column_ref[lax.rem(row + step + 7, 8)] for step in range(3)] + [tail]
    whole = jnp.concatenate(members, axis=0)
    for head in range(4):
        low = head * HEAD_DIM
        for group in range(4):
            out_ref[group * 4 + head, :, :HEAD_DIM] = whole[:, low : low + HEAD_DIM]
            out_ref[group * 4 + head, :, HEAD_DIM:] = whole[:, 512 + low : 512 + low + HEAD_DIM]


def prepare_kernel(own_ref, one_ref, two_ref, three_ref, *refs):
    x_ref, next_ref, prev_ref, query_ref, sems = refs
    copies = []
    for step, ref in enumerate((own_ref, one_ref, two_ref, three_ref)):
        begin = pl.multiple_of(other_place(step) * 128, 128)
        copies.append((ref, x_ref.at[pl.ds(begin, 128), :]))
    wait_copies(begin_copies(copies, sems))
    x = x_ref[...]
    next_ref[:64] = x[TOKENS - 64 :, HEAD_DIM:]
    prev_ref[:64] = x[:64, HEAD_DIM:]
    first = restrict(x, pair_sums(256, 512))
    next_ref[64:192] = first[128:, HEAD_DIM:]
    prev_ref[64:192] = first[:128, HEAD_DIM:]
    query_ref[:256] = first[:, :HEAD_DIM]
    second = restrict(first, pair_sums(128, 256))
    next_ref[192:] = second[:, HEAD_DIM:]
    prev_ref[192:] = second[:, HEAD_DIM:]
    query_ref[256:384] = second[:, :HEAD_DIM]
    third = restrict(second[:, :HEAD_DIM], pair_sums(64, 128))
    query_ref[384:448] = third
    fourth = restrict(third, pair_sums(32, 64))
    query_ref[448:480] = fourth
    fifth = restrict(fourth, pair_sums(16, 32))
    query_ref[480:496] = fifth
    query_ref[496:512] = restrict(fifth, pair_sums(16, 16))


def block_rows(array, blocks):
    return jnp.concatenate([array[block * BLOCK : (block + 1) * BLOCK] for block in blocks], axis=0)


def far_piece(query, pairs_ref, block, block_count, first=0):
    even = block % 2 == 0
    chosen = (
        jnp.where(even, block - 2, block - 3),
        jnp.where(even, block + 2, block - 2),
        jnp.where(even, block + 3, block + 2),
    )
    valid = [(target >= 0) & (target < block_count) for target in chosen]
    last = pairs_ref.shape[0] // BLOCK - 1
    parts = []
    for target in chosen:
        begin = pl.multiple_of(jnp.clip(target - first, 0, last) * BLOCK, BLOCK)
        parts.append(pairs_ref[pl.ds(begin, BLOCK), :])
    return attend(query, jnp.concatenate(parts, axis=0), third_mask(query.shape[0], valid))


def gather_levels(row, row_ref, third_ref, fourth_ref, fifth_ref, sixth_ref):
    wide, narrow = pair_sums(128, 256), pair_sums(64, 128)
    fifth_ref[...] = jnp.zeros_like(fifth_ref)
    for step in range(3):
        low, high = step * 256, step * 128
        rows = [row_ref[source, step * 16 : (step + 1) * 16] for source in range(16)]
        third = jnp.concatenate(rows, axis=0)
        third_ref[low : low + 256] = third
        fourth = restrict(third, wide)
        fourth_ref[high : high + 128] = fourth
        begin = pl.multiple_of(lax.rem(row + step + 7, 8) * 64, 64)
        fifth_ref[pl.ds(begin, 64), :] = restrict(fourth, narrow)
    tail = jnp.concatenate([row_ref[source, 48:64] for source in range(16)], axis=0)
    out_row = lax.broadcasted_iota(jnp.int32, (256, 256), 0)
    in_row = lax.broadcasted_iota(jnp.int32, (256, 256), 1)
    of_fifth = ((out_row & 63) >> 2) * 16 + (out_row >> 6) * 4 + (out_row & 3)
    of_sixth = ((out_row & 31) >> 1) * 16 + 12 + ((out_row >> 5) & 1) * 2 + (out_row & 1)
    source = jnp.where(out_row < 192, of_fifth, of_sixth)
    matrix = jnp.where(in_row == source, 1.0, 0.0).astype(jnp.bfloat16)
    ordered = jnp.dot(matrix, tail, preferred_element_type=jnp.float32).astype(jnp.bfloat16)
    for slot in range(3):
        begin = pl.multiple_of(needed_row(row, slot) * 64, 64)
        fifth_ref[pl.ds(begin, 64), :] = ordered[slot * 64 : (slot + 1) * 64]
    for begin in range(0, 256, 128):
        sixth_ref[begin : begin + 128] = restrict(fifth_ref[2 * begin : 2 * begin + 256], wide)
    begin = pl.multiple_of(needed_row(row, 3) * 32, 64)
    sixth_ref[pl.ds(begin, 64), :] = ordered[192:]


def inner_kernel(x_ref, inner_ref):
    x = x_ref[...]
    for block in range(1, 7):
        rows = slice(block * BLOCK, (block + 1) * BLOCK)
        keys = slice((block - 1) * BLOCK, (block + 2) * BLOCK)
        near = attend(x[rows, :HEAD_DIM], x[keys, HEAD_DIM:], None)
        for index, member in enumerate(near):
            inner_ref[index, rows] = member


def far_kernel(query_ref, row_hbm, far_ref, row_ref, *refs):
    *levels, scratch, sems = refs
    started = begin_copies(((row_hbm, row_ref),), sems)
    wait_copies(started)
    quad = my_quad()
    row = quad // 4
    third_ref, fourth_ref, fifth_ref, sixth_ref = levels
    gather_levels(row, row_ref, third_ref, fourth_ref, fifth_ref, sixth_ref)
    state = far_piece(query_ref[496:512], sixth_ref, row // 2, 4)
    state = spread(state, scratch, 8, 2)
    state = merge_pieces(far_piece(query_ref[480:496], fifth_ref, row, 8), state)
    state = spread(state, scratch, 16, 2)
    fourth = far_piece(query_ref[448:480], fourth_ref, quad // 2, 16, 2 * row - 2)
    state = spread(merge_pieces(fourth, state), scratch, 32, 2)
    third = far_piece(query_ref[384:448], third_ref, quad, 32, 4 * row - 4)
    for index, member in enumerate(merge_pieces(third, state)):
        for step in range(2):
            far_ref[index, pl.ds(step, 64, stride=2), :] = member


def attend_kernel(
    x_hbm, query_ref, far_ref, inner_hbm, prev_hbm, next_hbm, out_ref, *refs
):
    x_ref, inner_ref, prev_ref, next_ref, scratch, sems = refs
    copies = [(prev_hbm, prev_ref), (next_hbm, next_ref)]
    for part in range(4):
        rows = pl.ds(part * 128, 128)
        copies.append((x_hbm.at[rows], x_ref.at[rows]))
    for index in range(3):
        copies.append((inner_hbm.at[index], inner_ref.at[index]))
    wait_copies(begin_copies(copies, sems))
    quad = my_quad()
    has_prev = quad > 0
    has_next = quad < QUADS - 1
    x = x_ref[...]
    state = tuple(far_ref[index] for index in range(3))
    prev, later = prev_ref[...], next_ref[...]
    rim = jnp.concatenate([prev[192:], later[192:]], axis=0)
    pieces = []
    for block, chosen, valid in (
        (0, (0, 2, 3), (has_prev, has_next, has_next)),
        (1, (0, 1, 3), (has_prev, has_prev, has_next)),
    ):
        rows = slice(256 + block * BLOCK, 256 + (block + 1) * BLOCK)
        pieces.append(attend(query_ref[rows], block_rows(rim, chosen), third_mask(BLOCK, valid)))
    second = tuple(jnp.concatenate(members, axis=0) for members in zip(*pieces))
    state = spread(merge_pieces(second, state), scratch, 128, 2)
    own = restrict(x[:, HEAD_DIM:], pair_sums(256, 512))
    rim = jnp.concatenate([prev[64:192], own, later[64:192]], axis=0)
    pieces = []
    for block, chosen, valid in (
        (0, (0, 4, 5), (has_prev, True, True)),
        (1, (0, 1, 5), (has_prev, has_prev, True)),
        (2, (2, 6, 7), (True, has_next, has_next)),
        (3, (2, 3, 7), (True, True, has_next)),
    ):
        rows = slice(block * BLOCK, (block + 1) * BLOCK)
        pieces.append(attend(query_ref[rows], block_rows(rim, chosen), third_mask(BLOCK, valid)))
    first = tuple(jnp.concatenate(members, axis=0) for members in zip(*pieces))
    state = spread(merge_pieces(first, state), scratch, 256, 2)
    rim = jnp.concatenate([prev[:64], x[:, HEAD_DIM:], later[:64]], axis=0)
    for block in range(8):
        rows = slice(block * BLOCK, (block + 1) * BLOCK)
        if block in (0, 7):
            valid = (has_prev, True, True) if block == 0 else (True, True, has_next)
            keys = rim[block * BLOCK : (block + 3) * BLOCK]
            near = attend(x[rows, :HEAD_DIM], keys, third_mask(BLOCK, valid))
        else:
            near = tuple(inner_ref[index, rows] for index in range(3))
        _, total, summed = merge_pieces(near, tuple(member[rows] for member in state))
        out_ref[rows] = (summed / total).astype(jnp.bfloat16)


def project_kernel(attended_ref, weight_ref, gain_ref, out_ref):
    rows = jnp.concatenate([attended_ref[head] for head in range(4)], axis=1)
    widened = rows.astype(jnp.float32)
    squares = jnp.sum(widened * widened, axis=1, keepdims=True)
    squares = jnp.transpose(jnp.broadcast_to(squares, (128, 128)))[:16]
    coarse = squares.astype(jnp.bfloat16)
    rest = (squares - coarse.astype(jnp.float32)).astype(jnp.bfloat16)
    gained = (widened * gain_ref[...]).astype(jnp.bfloat16)
    for target in range(4):
        columns = slice(target * 512, (target + 1) * 512)
        product = jnp.dot(gained, weight_ref[:, columns], preferred_element_type=jnp.float32)
        out_ref[target, :128] = product.astype(jnp.bfloat16)
        out_ref[target, 128:, :128] = coarse
        out_ref[target, 128:, 128:256] = rest
        out_ref[target, 128:, 256:] = jnp.zeros((16, 256), jnp.bfloat16)


def sum_kernel(parts_ref, out_ref):
    summed = jnp.zeros((128, 512), jnp.float32)
    squares = jnp.zeros((16, 128), jnp.float32)
    for source in range(4):
        summed = summed + parts_ref[source, :128].astype(jnp.float32)
        squares = squares + parts_ref[source, 128:, :128].astype(jnp.float32)
        squares = squares + parts_ref[source, 128:, 128:256].astype(jnp.float32)
    mean_square = jnp.transpose(jnp.broadcast_to(squares[:1], (128, 128)))[:, :1] * (1.0 / 2048)
    out_ref[...] = (summed * lax.rsqrt(mean_square + eps_value)).astype(jnp.bfloat16)


def shift_pairs(by):
    return [
        (quad * 4 + place, (quad + by) * 4 + place)
        for quad in range(QUADS)
        if 0 <= quad + by < QUADS
        for place in range(4)
    ]


def exchange_pairs(step):
    return [(device, device ^ step) for device in range(4 * QUADS)]


ANYWHERE = pl.BlockSpec(memory_space=pl.ANY)
IN_HBM = pl.BlockSpec(memory_space=pltpu.HBM)


def vmem(count):
    return [pl.BlockSpec(memory_space=pltpu.VMEM)] * count


def bf16(*shape):
    return jax.ShapeDtypeStruct(shape, jnp.bfloat16)


def shards(queries, keys, values, norm_gain, out_weight):
    line = ("y", "zh", "zl", "c")
    column, *heads = pl.pallas_call(
        open_kernel,
        out_shape=[bf16(8, 16, 1024)] + [bf16(128, 3 * HEAD_DIM)] * 4,
        in_specs=[ANYWHERE] * 3,
        out_specs=vmem(5),
        scratch_shapes=[
            pltpu.VMEM((128, 1024), jnp.bfloat16),
            pltpu.SemaphoreType.DMA((14,)),
        ],
        compiler_params=FULL,
    )(queries, keys, values)
    column = lax.all_to_all(column, "y", 0, 0, tiled=True)
    for step in range(1, 4):
        heads[step] = lax.ppermute(heads[step], line, exchange_pairs(step))
    row_parts = pl.pallas_call(
        column_kernel,
        out_shape=bf16(16, 64, PAIR),
        in_specs=vmem(1) + [ANYWHERE] * 3,
        out_specs=vmem(1)[0],
        compiler_params=PARAMS,
    )(column, *heads[1:])
    row_all = lax.all_to_all(row_parts, ("zh", "zl", "c"), 0, 0, tiled=True)
    x, to_next, to_prev, coarse_queries = pl.pallas_call(
        prepare_kernel,
        out_shape=[
            bf16(TOKENS, 3 * HEAD_DIM),
            bf16(320, PAIR),
            bf16(320, PAIR),
            bf16(512, HEAD_DIM),
        ],
        in_specs=[ANYWHERE] * 4,
        out_specs=vmem(4),
        scratch_shapes=[pltpu.SemaphoreType.DMA((4,))],
        compiler_params=PARAMS,
    )(*heads)
    from_prev = lax.ppermute(to_next, line, shift_pairs(1))
    from_next = lax.ppermute(to_prev, line, shift_pairs(-1))
    inner = pl.pallas_call(
        inner_kernel,
        out_shape=jax.ShapeDtypeStruct((3, TOKENS, HEAD_DIM), jnp.float32),
        in_specs=vmem(1),
        out_specs=vmem(1)[0],
        compiler_params=PARAMS,
    )(x)
    far = pl.pallas_call(
        far_kernel,
        out_shape=jax.ShapeDtypeStruct((3, 128, HEAD_DIM), jnp.float32),
        in_specs=vmem(1) + [ANYWHERE],
        out_specs=vmem(1)[0],
        scratch_shapes=[
            pltpu.VMEM((16, 64, PAIR), jnp.bfloat16),
            pltpu.VMEM((768, PAIR), jnp.bfloat16),
            pltpu.VMEM((384, PAIR), jnp.bfloat16),
            pltpu.VMEM((512, PAIR), jnp.bfloat16),
            pltpu.VMEM((256, PAIR), jnp.bfloat16),
            pltpu.VMEM((3, 128, HEAD_DIM), jnp.float32),
            pltpu.SemaphoreType.DMA((1,)),
        ],
        compiler_params=PARAMS,
    )(coarse_queries, row_all)
    attended = pl.pallas_call(
        attend_kernel,
        out_shape=bf16(TOKENS, HEAD_DIM),
        in_specs=[IN_HBM] + vmem(2) + [IN_HBM] * 3,
        out_specs=vmem(1)[0],
        scratch_shapes=[
            pltpu.VMEM((TOKENS, 3 * HEAD_DIM), jnp.bfloat16),
            pltpu.VMEM((3, TOKENS, HEAD_DIM), jnp.float32),
            pltpu.VMEM((320, PAIR), jnp.bfloat16),
            pltpu.VMEM((320, PAIR), jnp.bfloat16),
            pltpu.VMEM((3, TOKENS, HEAD_DIM), jnp.float32),
            pltpu.SemaphoreType.DMA((9,)),
        ],
        compiler_params=PARAMS,
    )(x, coarse_queries, far, inner, from_prev, from_next)
    own = lax.all_to_all(attended.reshape(4, 128, HEAD_DIM), ("zl", "c"), 0, 0, tiled=True)
    products = pl.pallas_call(
        project_kernel,
        out_shape=bf16(4, 144, 512),
        in_specs=vmem(3),
        out_specs=vmem(1)[0],
        compiler_params=PARAMS,
    )(own, out_weight, norm_gain.reshape(1, 512))
    parts = lax.all_to_all(products, "x", 0, 0, tiled=True)
    return pl.pallas_call(
        sum_kernel,
        out_shape=bf16(128, 512),
        in_specs=vmem(1),
        out_specs=vmem(1)[0],
        compiler_params=PARAMS,
    )(parts)


def solution(mesh):
    grid = Mesh(mesh.devices.reshape(8, 4, 2, 2, 4), ("y", "zh", "zl", "c", "x"))
    split = P(("y", "zh", "zl", "c"), "x")
    return jax.shard_map(
        shards,
        mesh=grid,
        in_specs=(split, split, split, P("x"), P("x", None)),
        out_specs=split,
        check_vma=False,
    )
```

```python
import math

import jax
import jax.numpy as jnp
from jax import lax
from jax.experimental import pallas as pl
from jax.experimental.pallas import tpu as pltpu
from jax.sharding import Mesh
from jax.sharding import PartitionSpec as P

HEAD_DIM = 128
BLOCK = 64
QUADS = 32
TOKENS = 512
PAIR = 2 * HEAD_DIM
eps_value = 1e-06
inv_root = 1.0 / math.sqrt(2.0)
scaling = 1.0 / math.sqrt(HEAD_DIM)
NEG = -1e30
PARAMS = pltpu.CompilerParams(vmem_limit_bytes=48 * 1024 * 1024)
FULL = pltpu.CompilerParams(vmem_limit_bytes=60 * 1024 * 1024)
NEEDED = (
    (2, 3, 6, 4),
    (3, 6, 7, 4),
    (0, 4, 5, 6),
    (0, 1, 5, 6),
    (2, 6, 7, 0),
    (2, 3, 7, 0),
    (4, 0, 1, 2),
    (4, 5, 1, 2),
)


def pair_sums(rows, columns):
    out_row = lax.broadcasted_iota(jnp.int32, (rows, columns), 0)
    in_row = lax.broadcasted_iota(jnp.int32, (rows, columns), 1)
    return ((in_row >> 1) == out_row).astype(jnp.float32).astype(jnp.bfloat16)


def restrict(fine, matrix):
    summed = jnp.dot(matrix, fine, preferred_element_type=jnp.float32)
    return (summed * inv_root).astype(jnp.bfloat16)


def piece(query, key, value, allowed):
    scores = lax.dot_general(
        query, key, (((1,), (1,)), ((), ())), preferred_element_type=jnp.float32
    )
    scores = scores * scaling
    if allowed is not None:
        scores = jnp.where(allowed, scores, NEG)
    highest = jnp.max(scores, axis=1, keepdims=True)
    weights = jnp.exp(scores - highest)
    total = jnp.sum(weights, axis=1, keepdims=True)
    summed = jnp.dot(weights.astype(jnp.bfloat16), value, preferred_element_type=jnp.float32)
    shape = summed.shape
    return jnp.broadcast_to(highest, shape), jnp.broadcast_to(total, shape), summed


def attend(query, pairs, allowed):
    return piece(query, pairs[:, :HEAD_DIM], pairs[:, HEAD_DIM:], allowed)


def merge_pieces(current, incoming):
    largest = jnp.maximum(current[0], incoming[0])
    older = jnp.exp(current[0] - largest)
    newer = jnp.exp(incoming[0] - largest)
    return (
        largest,
        current[1] * older + incoming[1] * newer,
        current[2] * older + incoming[2] * newer,
    )


def spread(state, scratch, rows, factor):
    result = []
    for index, member in enumerate(state):
        for step in range(factor):
            scratch[index, pl.ds(step, rows, stride=factor), :] = member[:rows]
        result.append(scratch[index, : rows * factor, :])
    return tuple(result)


def third_mask(rows, valid):
    block = lax.broadcasted_iota(jnp.int32, (rows, 3 * BLOCK), 1) // BLOCK
    flags = [jnp.where(flag, 1, 0) for flag in valid]
    chosen = jnp.where(block == 0, flags[0], jnp.where(block == 1, flags[1], flags[2]))
    return chosen == 1


def needed_row(row, slot):
    chosen = NEEDED[0][slot]
    for index in range(1, 8):
        chosen = jnp.where(row == index, NEEDED[index][slot], chosen)
    return chosen


def my_quad():
    return lax.axis_index("y") * 4 + lax.axis_index("zh")


def begin_copies(copies, sems):
    started = [
        pltpu.make_async_copy(source, target, sems.at[index])
        for index, (source, target) in enumerate(copies)
    ]
    for copy in started:
        copy.start()
    return started


def wait_copies(started):
    for copy in started:
        copy.wait()


def other_place(step):
    high, low = lax.axis_index("zl"), lax.axis_index("c")
    if step & 2:
        high = 1 - high
    if step & 1:
        low = 1 - low
    return high * 2 + low


def open_kernel(queries_ref, keys_ref, values_ref, column_ref, *refs):
    head_refs, pairs_ref, sems = refs[:4], refs[4], refs[5]
    copies = [(keys_ref, pairs_ref.at[:, :512]), (values_ref, pairs_ref.at[:, 512:])]
    for step, head_ref in enumerate(head_refs):
        begin = pl.multiple_of(other_place(step) * HEAD_DIM, HEAD_DIM)
        for index, ref in enumerate((queries_ref, keys_ref, values_ref)):
            columns = slice(index * HEAD_DIM, (index + 1) * HEAD_DIM)
            copies.append((ref.at[:, pl.ds(begin, HEAD_DIM)], head_ref.at[:, columns]))
    started = begin_copies(copies, sems)
    wait_copies(started[:2])
    first = restrict(pairs_ref[...], pair_sums(64, 128))
    third = restrict(restrict(first, pair_sums(32, 64)), pair_sums(16, 32))
    for row in range(8):
        column_ref[row] = third
    wait_copies(started[2:])


def column_kernel(column_ref, *refs):
    out_ref = refs[-1]
    row = lax.axis_index("y")
    chosen = [needed_row(row, slot) for slot in range(4)]
    chosen.append(chosen[3] + 1)
    rest = jnp.concatenate([column_ref[source] for source in chosen], axis=0)
    fourth = restrict(rest, pair_sums(48, 80))
    fifth = restrict(fourth, pair_sums(32, 48))
    out_row = lax.broadcasted_iota(jnp.int32, (16, 32), 0)
    in_row = lax.broadcasted_iota(jnp.int32, (16, 32), 1)
    kept = (out_row < 12) & (in_row == out_row)
    halved = (out_row >= 12) & (((in_row - 12) >> 1) == out_row - 12)
    matrix = jnp.where(kept | halved, 1.0, 0.0).astype(jnp.bfloat16)
    tail = jnp.dot(matrix, fifth, preferred_element_type=jnp.float32)
    place = lax.broadcasted_iota(jnp.int32, tail.shape, 0)
    tail = jnp.where(place < 12, tail, tail * inv_root).astype(jnp.bfloat16)
    members = [column_ref[lax.rem(row + step + 7, 8)] for step in range(3)] + [tail]
    whole = jnp.concatenate(members, axis=0)
    for head in range(4):
        low = head * HEAD_DIM
        for group in range(4):
            out_ref[group * 4 + head, :, :HEAD_DIM] = whole[:, low : low + HEAD_DIM]
            out_ref[group * 4 + head, :, HEAD_DIM:] = whole[:, 512 + low : 512 + low + HEAD_DIM]


def prepare_kernel(own_ref, one_ref, two_ref, three_ref, *refs):
    x_ref, next_ref, prev_ref, query_ref, sems = refs
    copies = []
    for step, ref in enumerate((own_ref, one_ref, two_ref, three_ref)):
        begin = pl.multiple_of(other_place(step) * 128, 128)
        copies.append((ref, x_ref.at[pl.ds(begin, 128), :]))
    wait_copies(begin_copies(copies, sems))
    x = x_ref[...]
    next_ref[:64] = x[TOKENS - 64 :, HEAD_DIM:]
    prev_ref[:64] = x[:64, HEAD_DIM:]
    first = restrict(x, pair_sums(256, 512))
    next_ref[64:192] = first[128:, HEAD_DIM:]
    prev_ref[64:192] = first[:128, HEAD_DIM:]
    query_ref[:256] = first[:, :HEAD_DIM]
    second = restrict(first, pair_sums(128, 256))
    next_ref[192:] = second[:, HEAD_DIM:]
    prev_ref[192:] = second[:, HEAD_DIM:]
    query_ref[256:384] = second[:, :HEAD_DIM]
    third = restrict(second[:, :HEAD_DIM], pair_sums(64, 128))
    query_ref[384:448] = third
    fourth = restrict(third, pair_sums(32, 64))
    query_ref[448:480] = fourth
    fifth = restrict(fourth, pair_sums(16, 32))
    query_ref[480:496] = fifth
    query_ref[496:512] = restrict(fifth, pair_sums(16, 16))


def block_rows(array, blocks):
    return jnp.concatenate([array[block * BLOCK : (block + 1) * BLOCK] for block in blocks], axis=0)


def far_piece(query, pairs_ref, block, block_count, first=0):
    even = block % 2 == 0
    chosen = (
        jnp.where(even, block - 2, block - 3),
        jnp.where(even, block + 2, block - 2),
        jnp.where(even, block + 3, block + 2),
    )
    valid = [(target >= 0) & (target < block_count) for target in chosen]
    last = pairs_ref.shape[0] // BLOCK - 1
    parts = []
    for target in chosen:
        begin = pl.multiple_of(jnp.clip(target - first, 0, last) * BLOCK, BLOCK)
        parts.append(pairs_ref[pl.ds(begin, BLOCK), :])
    return attend(query, jnp.concatenate(parts, axis=0), third_mask(query.shape[0], valid))


def gather_levels(row, row_ref, third_ref, fourth_ref, fifth_ref, sixth_ref):
    wide, narrow = pair_sums(128, 256), pair_sums(64, 128)
    fifth_ref[...] = jnp.zeros_like(fifth_ref)
    for step in range(3):
        low, high = step * 256, step * 128
        rows = [row_ref[source, step * 16 : (step + 1) * 16] for source in range(16)]
        third = jnp.concatenate(rows, axis=0)
        third_ref[low : low + 256] = third
        fourth = restrict(third, wide)
        fourth_ref[high : high + 128] = fourth
        begin = pl.multiple_of(lax.rem(row + step + 7, 8) * 64, 64)
        fifth_ref[pl.ds(begin, 64), :] = restrict(fourth, narrow)
    tail = jnp.concatenate([row_ref[source, 48:64] for source in range(16)], axis=0)
    out_row = lax.broadcasted_iota(jnp.int32, (256, 256), 0)
    in_row = lax.broadcasted_iota(jnp.int32, (256, 256), 1)
    of_fifth = ((out_row & 63) >> 2) * 16 + (out_row >> 6) * 4 + (out_row & 3)
    of_sixth = ((out_row & 31) >> 1) * 16 + 12 + ((out_row >> 5) & 1) * 2 + (out_row & 1)
    source = jnp.where(out_row < 192, of_fifth, of_sixth)
    matrix = jnp.where(in_row == source, 1.0, 0.0).astype(jnp.bfloat16)
    ordered = jnp.dot(matrix, tail, preferred_element_type=jnp.float32).astype(jnp.bfloat16)
    for slot in range(3):
        begin = pl.multiple_of(needed_row(row, slot) * 64, 64)
        fifth_ref[pl.ds(begin, 64), :] = ordered[slot * 64 : (slot + 1) * 64]
    for begin in range(0, 256, 128):
        sixth_ref[begin : begin + 128] = restrict(fifth_ref[2 * begin : 2 * begin + 256], wide)
    begin = pl.multiple_of(needed_row(row, 3) * 32, 64)
    sixth_ref[pl.ds(begin, 64), :] = ordered[192:]


def inner_kernel(x_ref, inner_ref):
    x = x_ref[...]
    for block in range(1, 7):
        rows = slice(block * BLOCK, (block + 1) * BLOCK)
        keys = slice((block - 1) * BLOCK, (block + 2) * BLOCK)
        near = attend(x[rows, :HEAD_DIM], x[keys, HEAD_DIM:], None)
        for index, member in enumerate(near):
            inner_ref[index, rows] = member


def far_kernel(query_ref, row_hbm, later_hbm, far_ref, row_ref, *refs):
    del later_hbm
    *levels, scratch, sems = refs
    started = begin_copies(((row_hbm, row_ref),), sems)
    wait_copies(started)
    quad = my_quad()
    row = quad // 4
    third_ref, fourth_ref, fifth_ref, sixth_ref = levels
    gather_levels(row, row_ref, third_ref, fourth_ref, fifth_ref, sixth_ref)
    state = far_piece(query_ref[496:512], sixth_ref, row // 2, 4)
    state = spread(state, scratch, 8, 2)
    state = merge_pieces(far_piece(query_ref[480:496], fifth_ref, row, 8), state)
    state = spread(state, scratch, 16, 2)
    fourth = far_piece(query_ref[448:480], fourth_ref, quad // 2, 16, 2 * row - 2)
    state = spread(merge_pieces(fourth, state), scratch, 32, 2)
    third = far_piece(query_ref[384:448], third_ref, quad, 32, 4 * row - 4)
    for index, member in enumerate(merge_pieces(third, state)):
        for step in range(2):
            far_ref[index, pl.ds(step, 64, stride=2), :] = member


def attend_kernel(
    x_hbm, query_ref, far_ref, inner_hbm, prev_hbm, next_hbm, out_ref, *refs
):
    x_ref, inner_ref, prev_ref, next_ref, scratch, sems = refs
    copies = [(prev_hbm, prev_ref), (next_hbm, next_ref)]
    for part in range(4):
        rows = pl.ds(part * 128, 128)
        copies.append((x_hbm.at[rows], x_ref.at[rows]))
    for index in range(3):
        copies.append((inner_hbm.at[index], inner_ref.at[index]))
    wait_copies(begin_copies(copies, sems))
    quad = my_quad()
    has_prev = quad > 0
    has_next = quad < QUADS - 1
    x = x_ref[...]
    state = tuple(far_ref[index] for index in range(3))
    prev, later = prev_ref[...], next_ref[...]
    rim = jnp.concatenate([prev[192:], later[192:]], axis=0)
    pieces = []
    for block, chosen, valid in (
        (0, (0, 2, 3), (has_prev, has_next, has_next)),
        (1, (0, 1, 3), (has_prev, has_prev, has_next)),
    ):
        rows = slice(256 + block * BLOCK, 256 + (block + 1) * BLOCK)
        pieces.append(attend(query_ref[rows], block_rows(rim, chosen), third_mask(BLOCK, valid)))
    second = tuple(jnp.concatenate(members, axis=0) for members in zip(*pieces))
    state = spread(merge_pieces(second, state), scratch, 128, 2)
    own = restrict(x[:, HEAD_DIM:], pair_sums(256, 512))
    rim = jnp.concatenate([prev[64:192], own, later[64:192]], axis=0)
    pieces = []
    for block, chosen, valid in (
        (0, (0, 4, 5), (has_prev, True, True)),
        (1, (0, 1, 5), (has_prev, has_prev, True)),
        (2, (2, 6, 7), (True, has_next, has_next)),
        (3, (2, 3, 7), (True, True, has_next)),
    ):
        rows = slice(block * BLOCK, (block + 1) * BLOCK)
        pieces.append(attend(query_ref[rows], block_rows(rim, chosen), third_mask(BLOCK, valid)))
    first = tuple(jnp.concatenate(members, axis=0) for members in zip(*pieces))
    state = spread(merge_pieces(first, state), scratch, 256, 2)
    rim = jnp.concatenate([prev[:64], x[:, HEAD_DIM:], later[:64]], axis=0)
    for block in range(8):
        rows = slice(block * BLOCK, (block + 1) * BLOCK)
        if block in (0, 7):
            valid = (has_prev, True, True) if block == 0 else (True, True, has_next)
            keys = rim[block * BLOCK : (block + 3) * BLOCK]
            near = attend(x[rows, :HEAD_DIM], keys, third_mask(BLOCK, valid))
        else:
            near = tuple(inner_ref[index, rows] for index in range(3))
        _, total, summed = merge_pieces(near, tuple(member[rows] for member in state))
        out_ref[rows] = (summed / total).astype(jnp.bfloat16)


def project_kernel(attended_ref, weight_ref, gain_ref, out_ref):
    rows = jnp.concatenate([attended_ref[head] for head in range(4)], axis=1)
    widened = rows.astype(jnp.float32)
    squares = jnp.sum(widened * widened, axis=1, keepdims=True)
    squares = jnp.transpose(jnp.broadcast_to(squares, (128, 128)))[:16]
    coarse = squares.astype(jnp.bfloat16)
    rest = (squares - coarse.astype(jnp.float32)).astype(jnp.bfloat16)
    gained = (widened * gain_ref[...]).astype(jnp.bfloat16)
    for target in range(4):
        columns = slice(target * 512, (target + 1) * 512)
        product = jnp.dot(gained, weight_ref[:, columns], preferred_element_type=jnp.float32)
        out_ref[target, :128] = product.astype(jnp.bfloat16)
        out_ref[target, 128:, :128] = coarse
        out_ref[target, 128:, 128:256] = rest
        out_ref[target, 128:, 256:] = jnp.zeros((16, 256), jnp.bfloat16)


def sum_kernel(parts_ref, out_ref):
    summed = jnp.zeros((128, 512), jnp.float32)
    squares = jnp.zeros((16, 128), jnp.float32)
    for source in range(4):
        summed = summed + parts_ref[source, :128].astype(jnp.float32)
        squares = squares + parts_ref[source, 128:, :128].astype(jnp.float32)
        squares = squares + parts_ref[source, 128:, 128:256].astype(jnp.float32)
    mean_square = jnp.transpose(jnp.broadcast_to(squares[:1], (128, 128)))[:, :1] * (1.0 / 2048)
    out_ref[...] = (summed * lax.rsqrt(mean_square + eps_value)).astype(jnp.bfloat16)


def shift_pairs(by):
    return [
        (quad * 4 + place, (quad + by) * 4 + place)
        for quad in range(QUADS)
        if 0 <= quad + by < QUADS
        for place in range(4)
    ]


def exchange_pairs(step):
    return [(device, device ^ step) for device in range(4 * QUADS)]


ANYWHERE = pl.BlockSpec(memory_space=pl.ANY)
IN_HBM = pl.BlockSpec(memory_space=pltpu.HBM)


def vmem(count):
    return [pl.BlockSpec(memory_space=pltpu.VMEM)] * count


def bf16(*shape):
    return jax.ShapeDtypeStruct(shape, jnp.bfloat16)


def shards(queries, keys, values, norm_gain, out_weight):
    line = ("y", "zh", "zl", "c")
    column, *heads = pl.pallas_call(
        open_kernel,
        out_shape=[bf16(8, 16, 1024)] + [bf16(128, 3 * HEAD_DIM)] * 4,
        in_specs=[ANYWHERE] * 3,
        out_specs=vmem(5),
        scratch_shapes=[
            pltpu.VMEM((128, 1024), jnp.bfloat16),
            pltpu.SemaphoreType.DMA((14,)),
        ],
        compiler_params=FULL,
    )(queries, keys, values)
    column = lax.all_to_all(column, "y", 0, 0, tiled=True)
    for step in range(1, 4):
        heads[step] = lax.ppermute(heads[step], line, exchange_pairs(step))
    row_parts = pl.pallas_call(
        column_kernel,
        out_shape=bf16(16, 64, PAIR),
        in_specs=vmem(1) + [ANYWHERE] * 3,
        out_specs=vmem(1)[0],
        compiler_params=PARAMS,
    )(column, *heads[1:])
    row_all = lax.all_to_all(row_parts, ("zh", "zl", "c"), 0, 0, tiled=True)
    x, to_next, to_prev, coarse_queries = pl.pallas_call(
        prepare_kernel,
        out_shape=[
            bf16(TOKENS, 3 * HEAD_DIM),
            bf16(320, PAIR),
            bf16(320, PAIR),
            bf16(512, HEAD_DIM),
        ],
        in_specs=[ANYWHERE] * 4,
        out_specs=vmem(4),
        scratch_shapes=[pltpu.SemaphoreType.DMA((4,))],
        compiler_params=PARAMS,
    )(*heads)
    from_prev = lax.ppermute(to_next, line, shift_pairs(1))
    from_next = lax.ppermute(to_prev, line, shift_pairs(-1))
    inner = pl.pallas_call(
        inner_kernel,
        out_shape=jax.ShapeDtypeStruct((3, TOKENS, HEAD_DIM), jnp.float32),
        in_specs=vmem(1),
        out_specs=vmem(1)[0],
        compiler_params=PARAMS,
    )(x)
    far = pl.pallas_call(
        far_kernel,
        out_shape=jax.ShapeDtypeStruct((3, 128, HEAD_DIM), jnp.float32),
        in_specs=vmem(1) + [ANYWHERE] * 2,
        out_specs=vmem(1)[0],
        scratch_shapes=[
            pltpu.VMEM((16, 64, PAIR), jnp.bfloat16),
            pltpu.VMEM((768, PAIR), jnp.bfloat16),
            pltpu.VMEM((384, PAIR), jnp.bfloat16),
            pltpu.VMEM((512, PAIR), jnp.bfloat16),
            pltpu.VMEM((256, PAIR), jnp.bfloat16),
            pltpu.VMEM((3, 128, HEAD_DIM), jnp.float32),
            pltpu.SemaphoreType.DMA((1,)),
        ],
        compiler_params=PARAMS,
    )(coarse_queries, row_all, x)
    attended = pl.pallas_call(
        attend_kernel,
        out_shape=bf16(TOKENS, HEAD_DIM),
        in_specs=[IN_HBM] + vmem(2) + [IN_HBM] * 3,
        out_specs=vmem(1)[0],
        scratch_shapes=[
            pltpu.VMEM((TOKENS, 3 * HEAD_DIM), jnp.bfloat16),
            pltpu.VMEM((3, TOKENS, HEAD_DIM), jnp.float32),
            pltpu.VMEM((320, PAIR), jnp.bfloat16),
            pltpu.VMEM((320, PAIR), jnp.bfloat16),
            pltpu.VMEM((3, TOKENS, HEAD_DIM), jnp.float32),
            pltpu.SemaphoreType.DMA((9,)),
        ],
        compiler_params=PARAMS,
    )(x, coarse_queries, far, inner, from_prev, from_next)
    own = lax.all_to_all(attended.reshape(4, 128, HEAD_DIM), ("zl", "c"), 0, 0, tiled=True)
    products = pl.pallas_call(
        project_kernel,
        out_shape=bf16(4, 144, 512),
        in_specs=vmem(3),
        out_specs=vmem(1)[0],
        compiler_params=PARAMS,
    )(own, out_weight, norm_gain.reshape(1, 512))
    parts = lax.all_to_all(products, "x", 0, 0, tiled=True)
    return pl.pallas_call(
        sum_kernel,
        out_shape=bf16(128, 512),
        in_specs=vmem(1),
        out_specs=vmem(1)[0],
        compiler_params=PARAMS,
    )(parts)


def solution(mesh):
    grid = Mesh(mesh.devices.reshape(8, 4, 2, 2, 4), ("y", "zh", "zl", "c", "x"))
    split = P(("y", "zh", "zl", "c"), "x")
    return jax.shard_map(
        shards,
        mesh=grid,
        in_specs=(split, split, split, P("x"), P("x", None)),
        out_specs=split,
        check_vma=False,
    )
```
